32 devices in a mesh: dp: 4 (over y, x), fsdp: 8 (over z, core).
Axes of the slice: x: 2, y: 2, z: 4, core: 2. Of those that a mesh axis runs over, the one named last changes fastest.
Arguments:
- tokens: bfloat16 [24576, 1024], P(('dp', 'fsdp')), may hold values from -6 to 6
- segment_ids: int32 [24576], P(('dp', 'fsdp')), may hold values from 0 to 2, as said below
- out_grad: bfloat16 [24576, 1024], P(('dp', 'fsdp')), may hold values from -6 to 6
- norm_gain: bfloat16 [1024], P('fsdp'), may hold values from 0.5 to 1.5
- w_query: bfloat16 [1024, 512], P('fsdp'), may hold values from -0.1875 to 0.1875
- w_key: bfloat16 [1024, 512], P('fsdp'), may hold values from -0.1875 to 0.1875
- w_value: bfloat16 [1024, 1024], P('fsdp'), may hold values from -0.1875 to 0.1875
- w_rank_in: bfloat16 [1024, 16], P('fsdp'), may hold values from -0.1875 to 0.1875
- w_rank_out: bfloat16 [16, 512], P(None, 'fsdp'), may hold values from -0.75 to 0.75
- gate_bias: bfloat16 [512], P('fsdp'), may hold values from 0.3 to 8.5
- w_out_gate: bfloat16 [1024, 1024], P('fsdp'), may hold values from -0.1875 to 0.1875
- head_gain: bfloat16 [256], P('fsdp'), may hold values from 0.5 to 1.5
- w_output: bfloat16 [1024, 1024], P('fsdp'), may hold values from -0.375 to 0.375
- ffn_gain: bfloat16 [1024], P('fsdp'), may hold values from 0.5 to 1.5
- w_gate: bfloat16 [1024, 2816], P('fsdp'), may hold values from -0.1875 to 0.1875
- w_up: bfloat16 [1024, 2816], P('fsdp'), may hold values from -0.1875 to 0.1875
- w_down: bfloat16 [2816, 1024], P('fsdp'), may hold values from -0.21875 to 0.21875
Outputs:
- block_out: bfloat16 [24576, 1024], P(('dp', 'fsdp'))
- input_grad: float32 [24576, 1024], P(('dp', 'fsdp'))
- grad_norm_gain: float32 [1024], P('fsdp')
- grad_query: float32 [1024, 512], P('fsdp')
- grad_key: float32 [1024, 512], P('fsdp')
- grad_value: float32 [1024, 1024], P('fsdp')
- grad_rank_in: float32 [1024, 16], P('fsdp')
- grad_rank_out: float32 [16, 512], P(None, 'fsdp')
- grad_gate_bias: float32 [512], P('fsdp')
- grad_out_gate: float32 [1024, 1024], P('fsdp')
- grad_head_gain: float32 [256], P('fsdp')
- grad_output: float32 [1024, 1024], P('fsdp')
- grad_ffn_gain: float32 [1024], P('fsdp')
- grad_gate: float32 [1024, 2816], P('fsdp')
- grad_up: float32 [1024, 2816], P('fsdp')
- grad_down: float32 [2816, 1024], P('fsdp')
The draws below stay inside these ranges and needn't reach their ends.
Inputs may be any that keep to these rules, and one draw needn't show every extreme that they name: `segment_ids`: within each micro-batch stream of 3072 tokens the ids do not fall; document 0 ends after at least one token and strictly inside the stream's first 384 tokens, and document 2 begins strictly after the first of the stream's last 384 tokens, so document 1 runs from the first device of fsdp to the last and every change of id lies strictly inside one device's 384 tokens.
All inputs are finite; a program needn't handle non-finite values.
Results may differ from the reference program's by a relative error of at most 0.03.
Values may be sent and summed in bfloat16 or wider, within the bound.
A program may use at most 256 MiB of HBM per device.

```python
import jax
import jax.numpy as jnp
from jax import lax

D = 1024
HEADS = 4
DK = 128
DV = 256
RANK = 16
FF = 2816
STRETCH = 64
MICRO = 2
SLAB = 384
STREAM = 3072
TOKENS = 24576


def draw_segment_ids(key, part):
    key = jax.random.fold_in(key, 11)
    groups = TOKENS // (STREAM * MICRO)
    devices_per = STREAM // SLAB
    key_head, key_tail = jax.random.split(key)
    first_cut = jax.random.randint(key_head, (groups, MICRO, 1), 1, SLAB)
    last_cut = jax.random.randint(key_tail, (groups, MICRO, 1), 1, SLAB)
    places = jnp.arange(STREAM, dtype=jnp.int32)[None, None, :]
    ids = (places >= first_cut).astype(jnp.int32) + (places >= STREAM - last_cut).astype(jnp.int32)
    ids = ids.reshape(groups, MICRO, devices_per, SLAB).transpose(0, 2, 1, 3)
    return ids.reshape(TOKENS)


def draw_gate_bias(key, part):
    key = jax.random.fold_in(key, 23)
    key_pick, key_fast, key_slow = jax.random.split(key, 3)
    share = 0.5
    slow = jax.random.bernoulli(key_pick, share, (HEADS, 1))
    fast_values = jax.random.uniform(key_fast, (HEADS, DK), minval=0.3, maxval=1.5)
    slow_values = jax.random.uniform(key_slow, (HEADS, DK), minval=6.5, maxval=8.5)
    return jnp.where(slow, slow_values, fast_values).reshape(HEADS * DK).astype(jnp.bfloat16)


def shard_levels(own_key, extent, cuts, smallest, high):
    factor_of, own = 1.0, jax.random.fold_in(own_key, 6)
    for axis_at, blocks in cuts:
        heights = jnp.exp(jax.random.uniform(jax.random.fold_in(own, axis_at), (blocks,), jnp.float32, smallest / len(cuts), high / len(cuts)))
        factor_of = factor_of * jnp.repeat(heights, extent[axis_at] // blocks).reshape([-1 if axis == axis_at else 1 for axis in range(len(extent))])
    return factor_of


def centred(rng, dims, scale, limit, shards=(), kind=jnp.bfloat16):
    drawn = jax.random.normal(rng, dims, jnp.float32) * scale
    if len(shards) > 0:
        drawn = shard_levels(rng, dims, shards, -0.22, 0.18) * drawn
    return jnp.clip(drawn, min=-limit, max=limit).astype(kind)


def setup_inputs(seed: int = 0) -> dict:
    splits = jax.random.split(jax.random.key(seed), 18)
    tokens = centred(splits[0], (TOKENS, D), 1.0, 6.0, ((0, 32),))
    segment_ids = draw_segment_ids(jax.random.fold_in(splits[17], 71), 0)
    out_grad = centred(splits[2], (TOKENS, D), 1.0, 6.0, ((0, 32),))
    norm_gain = jnp.clip(1.0 + 0.1 * jax.random.normal(splits[3], (D,), jnp.float32), 0.5, 1.5).astype(jnp.bfloat16)
    w_query = centred(splits[4], (D, HEADS * DK), D ** -0.5, 0.1875, ((0, 8),))
    w_key = centred(splits[5], (D, HEADS * DK), D ** -0.5, 0.1875, ((0, 8),))
    w_value = centred(splits[6], (D, HEADS * DV), D ** -0.5, 0.1875, ((0, 8),))
    w_rank_in = centred(splits[7], (D, RANK), D ** -0.5, 0.1875, ((0, 8),))
    w_rank_out = centred(splits[8], (RANK, HEADS * DK), (4 * RANK) ** -0.5, 0.75, ((1, 8),))
    gate_bias = draw_gate_bias(jax.random.fold_in(splits[17], 71), 0)
    w_out_gate = centred(splits[10], (D, HEADS * DV), D ** -0.5, 0.1875, ((0, 8),))
    head_gain = jnp.clip(1.0 + 0.1 * jax.random.normal(splits[11], (DV,), jnp.float32), 0.5, 1.5).astype(jnp.bfloat16)
    w_output = centred(splits[12], (HEADS * DV, D), (HEADS * DV // 4) ** -0.5, 0.375, ((0, 8),))
    ffn_gain = jnp.clip(1.0 + 0.1 * jax.random.normal(splits[13], (D,), jnp.float32), 0.5, 1.5).astype(jnp.bfloat16)
    w_gate = centred(splits[14], (D, FF), D ** -0.5, 0.1875, ((0, 8),))
    w_up = centred(splits[15], (D, FF), D ** -0.5, 0.1875, ((0, 8),))
    w_down = centred(splits[16], (FF, D), (FF // 4) ** -0.5, 0.21875, ((0, 8),))
    return {"tokens": tokens, "segment_ids": segment_ids, "out_grad": out_grad, "norm_gain": norm_gain, "w_query": w_query, "w_key": w_key, "w_value": w_value, "w_rank_in": w_rank_in, "w_rank_out": w_rank_out, "gate_bias": gate_bias, "w_out_gate": w_out_gate, "head_gain": head_gain, "w_output": w_output, "ffn_gain": ffn_gain, "w_gate": w_gate, "w_up": w_up, "w_down": w_down}


precise = lax.Precision.HIGHEST
eps_norm = 1e-06
eps_head = 0.1

@jax.custom_vjp
def low(v):
    return lax.optimization_barrier(v.astype(jnp.bfloat16)).astype(jnp.float32)

@jax.custom_vjp
def low_back(v):
    return v

def low_keep(v):
    return (low(v), None)

def low_pass(kept, grad):
    return (grad,)

def back_keep(v):
    return (v, None)

def back_low(kept, grad):
    return (low(grad),)
low.defvjp(low_keep, low_pass)
low_back.defvjp(back_keep, back_low)

def exact_dot(left, right):
    return jnp.dot(left, right, precision=precise, preferred_element_type=jnp.float32)

def block_step(carry, block):
    state, previous = carry
    q_block, k_block, v_block, g_block, s_block = block
    cumul = jnp.cumsum(g_block, axis=0)
    width = s_block.shape[0]
    places = jnp.arange(width, dtype=jnp.int32)
    causal = (places[:, None] >= places[None, :]) & (s_block[:, None] == s_block[None, :])
    spread = cumul[:, None] - cumul[None, :]
    spread = jnp.where(causal[:, :, None, None], spread, 0.0)
    factor = jnp.where(causal[:, :, None, None], jnp.exp(spread), 0.0)
    scores = jnp.einsum('ihc,jhc,ijhc->hij', q_block, k_block, factor, precision=precise)
    inner = jnp.einsum('hij,jhv->ihv', scores, v_block, precision=precise)
    keep = (s_block == previous).astype(jnp.float32)
    carried = jnp.einsum('ihc,hcv->ihv', q_block * jnp.exp(cumul) * keep[:, None, None], state, precision=precise)
    final_id = s_block[width - 1].astype(jnp.int32)
    tail = jnp.exp(cumul[width - 1][None] - cumul) * (s_block == final_id).astype(jnp.float32)[:, None, None]
    fresh = jnp.einsum('jhc,jhv->hcv', k_block * tail, v_block, precision=precise)
    new_state = keep[width - 1] * jnp.exp(cumul[width - 1])[:, :, None] * state + fresh
    return ((new_state, final_id), inner + carried)

def gla_core(queries, keys_in, values, log_gate, seg, state_start, prev_start):
    length = queries.shape[0]
    count = length // STRETCH
    blocks = (queries.reshape(count, STRETCH, HEADS, -1), keys_in.reshape(count, STRETCH, HEADS, -1), values.reshape(count, STRETCH, HEADS, -1), log_gate.reshape(count, STRETCH, HEADS, -1), seg.reshape(count, STRETCH).astype(jnp.int32))
    (state, last_id), output = lax.scan(jax.checkpoint(block_step), (state_start, prev_start), blocks)
    return (output.reshape(length, HEADS, -1), state)

def stream_forward(weights, inputs, seg):
    norm_gain, w_query, w_key, w_value, w_rank_in, w_rank_out, gate_bias, w_out_gate, head_gain, w_output, ffn_gain, w_gate, w_up, w_down = weights
    length = inputs.shape[0]
    scale_one = lax.rsqrt(lax.optimization_barrier(jnp.mean(inputs * inputs, axis=-1, keepdims=True)) + eps_norm)
    normed = low(low_back(inputs * scale_one * norm_gain))
    queries = low(low_back(exact_dot(normed, w_query)))
    keys_in = low(low_back(exact_dot(normed, w_key)))
    values = low(low_back(exact_dot(normed, w_value)))
    rank_mid = low(low_back(exact_dot(normed, w_rank_in)))
    gate_pre = low_back(exact_dot(rank_mid, w_rank_out)) + gate_bias
    log_gate = jax.nn.log_sigmoid(gate_pre) / 16.0
    out_gate = low_back(exact_dot(normed, w_out_gate))
    q_heads = queries.reshape(length, HEADS, -1) * DK ** (-0.5)
    k_heads = keys_in.reshape(length, HEADS, -1)
    v_heads = values.reshape(length, HEADS, -1)
    g_heads = log_gate.reshape(length, HEADS, -1)
    start = jnp.zeros((HEADS, k_heads.shape[2], v_heads.shape[2]), jnp.float32)
    attended, final_state = gla_core(q_heads, k_heads, v_heads, g_heads, seg, start, jnp.array(-1, jnp.int32))
    head_scale = lax.rsqrt(lax.optimization_barrier(jnp.mean(attended * attended, axis=-1, keepdims=True)) + eps_head)
    mixed = (attended * head_scale * head_gain).reshape(length, -1) * jax.nn.silu(out_gate)
    mixed = low(low_back(mixed))
    middle = inputs + low_back(exact_dot(mixed, w_output))
    scale_two = lax.rsqrt(lax.optimization_barrier(jnp.mean(middle * middle, axis=-1, keepdims=True)) + eps_norm)
    normed_two = low(low_back(middle * scale_two * ffn_gain))
    gate = low_back(exact_dot(normed_two, w_gate))
    upward = low_back(exact_dot(normed_two, w_up))
    hidden = low(low_back(jax.nn.silu(gate) * upward))
    return middle + low_back(exact_dot(hidden, w_down))

def reference(tokens, segment_ids, out_grad, norm_gain, w_query, w_key, w_value, w_rank_in, w_rank_out, gate_bias, w_out_gate, head_gain, w_output, ffn_gain, w_gate, w_up, w_down):
    weights = (norm_gain.astype(jnp.float32), w_query.astype(jnp.float32), w_key.astype(jnp.float32), w_value.astype(jnp.float32), w_rank_in.astype(jnp.float32), w_rank_out.astype(jnp.float32), gate_bias.astype(jnp.float32), w_out_gate.astype(jnp.float32), head_gain.astype(jnp.float32), w_output.astype(jnp.float32), ffn_gain.astype(jnp.float32), w_gate.astype(jnp.float32), w_up.astype(jnp.float32), w_down.astype(jnp.float32))
    groups = TOKENS // (STREAM * MICRO)
    devices_per = STREAM // SLAB

    def arrange(array):
        rest = array.shape[1:]
        shaped = array.reshape((groups, devices_per, MICRO, SLAB) + rest)
        shaped = jnp.swapaxes(shaped, 1, 2)
        return shaped.reshape((groups * MICRO, STREAM) + rest)

    def restore(array):
        rest = array.shape[2:]
        shaped = array.reshape((groups, MICRO, devices_per, SLAB) + rest)
        shaped = jnp.swapaxes(shaped, 1, 2)
        return shaped.reshape((TOKENS,) + rest)
    inputs_all = arrange(tokens.astype(jnp.float32))
    seg_all = arrange(segment_ids.astype(jnp.int32))
    cot_all = arrange(out_grad.astype(jnp.float32))
    zero = jax.tree.map(jnp.zeros_like, weights)

    def one_stream(total, item):
        inputs, seg, cotangent = item

        def forward(params, values_in):
            return stream_forward(params, values_in, seg)
        output, pull = jax.vjp(forward, weights, inputs)
        grad_weights, grad_inputs = pull(cotangent)
        return (jax.tree.map(jnp.add, total, grad_weights), (output, grad_inputs))
    total, (outputs, grad_inputs) = lax.scan(one_stream, zero, (inputs_all, seg_all, cot_all))
    return (restore(outputs).astype(jnp.bfloat16), restore(grad_inputs), total[0], total[1], total[2], total[3], total[4], total[5], total[6], total[7], total[8], total[9], total[10], total[11], total[12], total[13])
```

```python
import functools

import jax
import jax.numpy as jnp
import numpy as np
from jax import lax
from jax.experimental import pallas as pl
from jax.experimental.pallas import tpu as pltpu
from jax.sharding import PartitionSpec as P

HEADS = 4
DK = 128
DV = 256
SLAB = 384
CHUNK = 128
LEVELS = 7
SCALE = DK ** (-0.5)

eps_norm = 1e-06
eps_head = 0.1
bf16 = jnp.bfloat16
f32 = jnp.float32


def nn(left, right):
    return lax.dot_general(
        left.astype(bf16), right.astype(bf16), (((1,), (0,)), ((), ())), preferred_element_type=f32
    )


def tn(left, right):
    return lax.dot_general(
        left.astype(bf16), right.astype(bf16), (((0,), (0,)), ((), ())), preferred_element_type=f32
    )


def nt(left, right):
    return lax.dot_general(
        left.astype(bf16), right.astype(bf16), (((1,), (1,)), ((), ())), preferred_element_type=f32
    )


def rounded(values):
    return lax.optimization_barrier(values.astype(bf16)).astype(f32)


def rms_scale(values, gain):
    return values * lax.rsqrt(jnp.mean(values * values, axis=-1, keepdims=True) + eps_norm) * gain


def head_mix(attended, out_gate, head_gain):
    length = attended.shape[0]
    head_scale = lax.rsqrt(jnp.mean(attended * attended, axis=-1, keepdims=True) + eps_head)
    return (attended * head_scale * head_gain).reshape(length, -1) * jax.nn.silu(out_gate)


def swiglu(gate, upward):
    return jax.nn.silu(gate) * upward


def span_matrix():
    i = np.arange(CHUNK)[:, None]
    s = np.arange(CHUNK)[None, :]
    rows = []
    for level in range(LEVELS):
        half = 1 << level
        mid = (i // (2 * half)) * 2 * half + half - 1
        second = (i >> level) & 1 == 1
        rows.append(np.where(second, (s > mid) & (s <= i), (s > i) & (s <= mid)))
    rows.append(s <= i)
    rows.append(s > i)
    return np.concatenate(rows, axis=0).astype(np.float32)


def part(level):
    return slice(level * CHUNK, (level + 1) * CHUNK)


def chunk_factors(spans, g):
    high = g.astype(bf16)
    low = g - high.astype(f32)
    return jnp.exp(nn(spans, high) + nn(spans, low))


def iotas():
    return (
        lax.broadcasted_iota(jnp.int32, (CHUNK, CHUNK), 0),
        lax.broadcasted_iota(jnp.int32, (CHUNK, CHUNK), 1),
    )


def second_half(level, rows):
    return ((rows >> level) & 1) == 1


def meets(level, rows, columns):
    return ((rows >> (level + 1)) == (columns >> (level + 1))) & (
        (rows >> level) != (columns >> level)
    )


def chunk_scores(q, k, factors, same, rows, columns):
    scores = jnp.where(rows == columns, jnp.sum(q * k, axis=1, keepdims=True), 0.0)
    for level in range(LEVELS):
        mixed = (jnp.where(second_half(level, rows), q, k) * factors[part(level)]).astype(bf16)
        scores = scores + jnp.where(
            meets(level, rows, columns) & (rows > columns), nt(mixed, mixed), 0.0
        )
    return scores * same


def ahead_kernel(
    spans_ref,
    q_ref,
    k_ref,
    v_ref,
    g_ref,
    same_ref,
    keep_ref,
    tail_ref,
    out_ref,
    reach_ref,
    enter_ref,
    enter_coef_ref,
    last_ref,
    coef_ref,
    state,
    decay,
):
    step = pl.program_id(2)

    @pl.when(step == 0)
    def _():
        state[...] = jnp.zeros_like(state)
        decay[...] = jnp.ones_like(decay)

    rows, columns = iotas()
    q = q_ref[...].astype(f32) * SCALE
    k = k_ref[...].astype(f32)
    v = v_ref[...]
    factors = chunk_factors(spans_ref[...], g_ref[...])
    scores = chunk_scores(q, k, factors, same_ref[...].astype(f32), rows, columns)
    carry = factors[part(LEVELS)] * keep_ref[...].astype(f32)
    reach = q * carry
    tail = k * factors[part(LEVELS + 1)] * tail_ref[...].astype(f32)
    before = state[...]
    entering = decay[0:1, :]
    enter_ref[...] = before
    enter_coef_ref[...] = decay[...]
    out_ref[...] = nn(scores, v) + nt(reach, before)
    reach_ref[...] = (reach * entering).astype(bf16)
    coef = carry[CHUNK - 1 : CHUNK, :]
    after = before * coef + tn(v, tail)
    state[...] = after
    decay[...] = decay[...] * coef
    last_ref[...] = after
    coef_ref[...] = decay[...]


def behind_kernel(
    spans_ref,
    q_ref,
    k_ref,
    v_ref,
    g_ref,
    same_ref,
    keep_ref,
    tail_ref,
    enter_ref,
    enter_coef_ref,
    first_ref,
    grad_ref,
    end_ref,
    dq_ref,
    dk_ref,
    dv_ref,
    dg_ref,
    state,
    spread,
):
    step = pl.program_id(2)

    @pl.when(step == 0)
    def _():
        state[...] = end_ref[...]

    rows, columns = iotas()
    q = q_ref[...].astype(f32) * SCALE
    k = k_ref[...].astype(f32)
    v = v_ref[...]
    same = same_ref[...].astype(f32)
    factors = chunk_factors(spans_ref[...], g_ref[...])
    scores = chunk_scores(q, k, factors, same, rows, columns)
    carry = factors[part(LEVELS)] * keep_ref[...].astype(f32)
    reach = q * carry
    leave = factors[part(LEVELS + 1)] * tail_ref[...].astype(f32)
    tail = k * leave
    coef = carry[CHUNK - 1 : CHUNK, :]
    before = enter_ref[...] + enter_coef_ref[0:1, :] * first_ref[...]
    d_out = grad_ref[...].astype(bf16)
    d_after = state[...]

    d_scores = nt(d_out, v) * same
    dv_ref[...] = (tn(scores, d_out) + nt(tail, d_after)).astype(bf16)
    d_reach = nn(d_out, before)
    d_tail = nn(v, d_after)
    d_coef = jnp.sum(d_after * before, axis=0, keepdims=True)
    state[...] = coef * d_after + tn(d_out, reach)

    below = jnp.where(rows > columns, d_scores, 0.0)
    both = below + below.T
    diagonal = jnp.sum(jnp.where(rows == columns, d_scores, 0.0), axis=1, keepdims=True)
    d_q = diagonal * k + d_reach * carry
    d_k = diagonal * q + d_tail * leave
    for level in range(LEVELS):
        second = second_half(level, rows)
        factor = factors[part(level)]
        mixed = jnp.where(second, q, k) * factor
        d_mixed = nn(jnp.where(meets(level, rows, columns), both, 0.0), mixed)
        spread[part(level), :] = (d_mixed * mixed).astype(bf16)
        d_base = d_mixed * factor
        d_q = d_q + jnp.where(second, d_base, 0.0)
        d_k = d_k + jnp.where(second, 0.0, d_base)
    ending = jnp.where(rows == CHUNK - 1, d_coef * coef, 0.0)
    spread[part(LEVELS), :] = (d_reach * reach + ending).astype(bf16)
    spread[part(LEVELS + 1), :] = (d_tail * tail).astype(bf16)
    dg_ref[...] = tn(spans_ref[...], spread[...])
    dq_ref[...] = (d_q * SCALE).astype(bf16)
    dk_ref[...] = d_k.astype(bf16)


def core_specs(chunks, turn):
    def at(m, c):
        return m * chunks + turn(c)

    key = pl.BlockSpec((CHUNK, DK), lambda m, h, c: (at(m, c), h))
    value = pl.BlockSpec((CHUNK, DV), lambda m, h, c: (at(m, c), h))
    plain = pl.BlockSpec((CHUNK, CHUNK), lambda m, h, c: (at(m, c), 0))
    spans = pl.BlockSpec(((LEVELS + 2) * CHUNK, CHUNK), lambda m, h, c: (0, 0))
    enter = pl.BlockSpec((None, None, DV, DK), lambda m, h, c: (at(m, c), h, 0, 0))
    enter_coef = pl.BlockSpec((None, None, 8, DK), lambda m, h, c: (at(m, c), h, 0, 0))
    ends = pl.BlockSpec((None, None, DV, DK), lambda m, h, c: (m, h, 0, 0))
    coef = pl.BlockSpec((None, None, 8, DK), lambda m, h, c: (m, h, 0, 0))
    return key, value, plain, spans, enter, enter_coef, ends, coef


LIMIT = 32 * 1024 * 1024


def core_ahead(spans, q, k, v, g, same, keep, tail):
    total = q.shape[0]
    micro, chunks = total // SLAB, SLAB // CHUNK
    key, value, plain, span, enter, enter_coef, ends, coef = core_specs(chunks, lambda c: c)
    return pl.pallas_call(
        ahead_kernel,
        grid=(micro, HEADS, chunks),
        in_specs=[span, key, key, value, key, plain, plain, plain],
        out_specs=[value, key, enter, enter_coef, ends, coef],
        out_shape=[
            jax.ShapeDtypeStruct((total, HEADS * DV), f32),
            jax.ShapeDtypeStruct((total, HEADS * DK), bf16),
            jax.ShapeDtypeStruct((micro * chunks, HEADS, DV, DK), f32),
            jax.ShapeDtypeStruct((micro * chunks, HEADS, 8, DK), f32),
            jax.ShapeDtypeStruct((micro, HEADS, DV, DK), f32),
            jax.ShapeDtypeStruct((micro, HEADS, 8, DK), f32),
        ],
        scratch_shapes=[pltpu.VMEM((DV, DK), f32), pltpu.VMEM((8, DK), f32)],
        compiler_params=pltpu.CompilerParams(vmem_limit_bytes=LIMIT),
        cost_estimate=pl.CostEstimate(
            flops=12 * total * HEADS * 9 * CHUNK * DK // 2, bytes_accessed=20 * 2**20, transcendentals=0
        ),
        name="core_ahead",
    )(spans, q, k, v, g, same, keep, tail)


def core_behind(spans, q, k, v, g, same, keep, tail, enters, enter_coefs, first, d_out, d_end):
    total = q.shape[0]
    micro, chunks = total // SLAB, SLAB // CHUNK
    key, value, plain, span, enter, enter_coef, ends, coef = core_specs(
        chunks, lambda c: chunks - 1 - c
    )
    return pl.pallas_call(
        behind_kernel,
        grid=(micro, HEADS, chunks),
        in_specs=[span, key, key, value, key, plain, plain, plain]
        + [enter, enter_coef, ends, value, ends],
        out_specs=[key, key, value, key],
        out_shape=[
            jax.ShapeDtypeStruct((total, HEADS * DK), bf16),
            jax.ShapeDtypeStruct((total, HEADS * DK), bf16),
            jax.ShapeDtypeStruct((total, HEADS * DV), bf16),
            jax.ShapeDtypeStruct((total, HEADS * DK), f32),
        ],
        scratch_shapes=[
            pltpu.VMEM((DV, DK), f32),
            pltpu.VMEM(((LEVELS + 2) * CHUNK, DK), bf16),
        ],
        compiler_params=pltpu.CompilerParams(vmem_limit_bytes=LIMIT),
        cost_estimate=pl.CostEstimate(
            flops=24 * total * HEADS * 9 * CHUNK * DK // 2, bytes_accessed=24 * 2**20, transcendentals=0
        ),
        name="core_behind",
    )(spans, q, k, v, g, same, keep, tail, enters, enter_coefs, first, d_out, d_end)


def split_masks(seg, joined):
    micro = seg.shape[0] // SLAB
    chunks = SLAB // CHUNK
    rows = seg.reshape(micro, chunks, CHUNK)
    first = rows[:, 0, 0]
    enter_id = jnp.concatenate(
        [jnp.where(joined, first, -1)[:, None], rows[:, :-1, CHUNK - 1]], axis=1
    )
    keep = rows == enter_id[:, :, None]
    tail = rows == rows[:, :, CHUNK - 1 :]
    same = rows[:, :, :, None] == rows[:, :, None, :]

    def wide(mask):
        return jnp.broadcast_to(mask.astype(bf16).reshape(-1, 1), (seg.shape[0], DK))

    return same.astype(bf16).reshape(-1, CHUNK), wide(keep), wide(tail)


def gathered_rows(x):
    return lax.all_gather(x, "fsdp", axis=0, tiled=True)


def scattered(x):
    return lax.psum_scatter(x.astype(bf16), "fsdp", scatter_dimension=0, tiled=True)


def across(x):
    return lax.psum(x, "dp").astype(f32)


def on_device(
    tokens,
    segment_ids,
    out_grad,
    norm_gain,
    w_query,
    w_key,
    w_value,
    w_rank_in,
    w_rank_out,
    gate_bias,
    w_out_gate,
    head_gain,
    w_output,
    ffn_gain,
    w_gate,
    w_up,
    w_down,
):
    total = tokens.shape[0]
    micro = total // SLAB
    count, place = lax.axis_size("fsdp"), lax.axis_index("fsdp")
    owned_rows = norm_gain.shape[0]
    nq, nv, rank = w_query.shape[1], w_value.shape[1], w_rank_in.shape[1]
    ff = w_gate.shape[1]
    wide_rank = 128
    spans = jnp.asarray(span_matrix(), bf16)

    sizes = [a.size for a in (norm_gain, gate_bias, head_gain, ffn_gain, w_rank_out)]
    cuts = np.cumsum([0] + sizes)
    small = jnp.concatenate(
        [norm_gain, gate_bias, head_gain, ffn_gain, w_rank_out.reshape(-1)]
    )
    small = lax.all_gather(small, "fsdp", axis=0)
    full_norm, full_bias, full_head, full_ffn = (
        small[:, cuts[n] : cuts[n + 1]].reshape(-1) for n in range(4)
    )
    full_rank_out = (
        small[:, cuts[4] : cuts[5]].reshape(count, rank, -1).transpose(1, 0, 2).reshape(rank, -1)
    )
    project = gathered_rows(
        jnp.concatenate(
            [w_query, w_key, w_value, w_out_gate, jnp.pad(w_rank_in, ((0, 0), (0, wide_rank - rank)))],
            axis=1,
        )
    )
    project, w_output, w_gate, w_up, w_down = lax.optimization_barrier(
        (project, w_output, w_gate, w_up, w_down)
    )
    full_output = gathered_rows(w_output)
    full_pair = gathered_rows(jnp.concatenate([w_gate, w_up], axis=1))
    full_down = gathered_rows(w_down)

    inputs = tokens.astype(f32)
    gain_one = full_norm.astype(f32)
    normed = rms_scale(inputs, gain_one).astype(bf16)
    qkv = nn(normed, project[:, : 2 * nq + nv]).astype(bf16)
    queries, keys_in, values = qkv[:, :nq], qkv[:, nq : 2 * nq], qkv[:, 2 * nq :]
    rest = nn(normed, project[:, 2 * nq + nv :])
    out_gate = rest[:, :nv]
    rank_mid = rest[:, nv : nv + rank].astype(bf16)
    gate_pre = nn(rank_mid, full_rank_out) + full_bias.astype(f32)
    log_gate = jax.nn.log_sigmoid(gate_pre) / 16.0

    same, keep, tail = split_masks(segment_ids, place > 0)
    local_out, reach, enters, enter_coefs, local_state, coef = core_ahead(
        spans, queries, keys_in, values, log_gate, same, keep, tail
    )
    coef = coef[:, :, 0, :]
    high = lax.optimization_barrier(coef.astype(bf16))
    low = (coef - high.astype(f32)).astype(bf16)
    lines = micro * HEADS
    parcel = jnp.concatenate(
        [local_state.astype(bf16).reshape(-1, DK), high.reshape(-1, DK), low.reshape(-1, DK)], axis=0
    )
    parcel = lax.all_gather(parcel, "fsdp", axis=0)
    states = parcel[:, : lines * DV].reshape(count, micro, HEADS, DV, DK)
    coefs = (
        parcel[:, lines * DV : lines * (DV + 1)].astype(f32)
        + parcel[:, lines * (DV + 1) :].astype(f32)
    ).reshape(count, micro, HEADS, 1, DK)
    state_in = jnp.zeros((micro, HEADS, DV, DK), f32)
    for k in range(count - 1):
        state_in = jnp.where(k < place, coefs[k] * state_in + states[k].astype(f32), state_in)
    reach_heads = reach.reshape(micro, SLAB, HEADS, DK)
    carried = jnp.einsum(
        "mthc,mhvc->mthv", reach_heads, state_in.astype(bf16), preferred_element_type=f32
    )
    attended = local_out.reshape(total, HEADS, DV) + carried.reshape(total, HEADS, DV)
    gain_head = full_head.astype(f32)
    mixed = head_mix(attended, out_gate, gain_head).astype(bf16)
    middle = inputs + nn(mixed, full_output)
    gain_two = full_ffn.astype(f32)
    normed_two = rms_scale(middle, gain_two).astype(bf16)
    gate = nn(normed_two, full_pair[:, :ff])
    upward = nn(normed_two, full_pair[:, ff:])
    hidden = swiglu(gate, upward).astype(bf16)
    block_out = (middle + nn(hidden, full_down)).astype(bf16)

    d_branch = out_grad
    o_down = scattered(tn(hidden, d_branch))
    d_hidden = rounded(nt(d_branch, full_down))
    _, pull = jax.vjp(swiglu, gate, upward)
    d_pair = jnp.concatenate([a.astype(bf16) for a in pull(d_hidden)], axis=1)
    o_pair = scattered(tn(normed_two, d_pair))
    d_normed_two = rounded(nt(d_pair, full_pair))
    _, pull = jax.vjp(rms_scale, middle, gain_two)
    d_middle_part, g_ffn = pull(d_normed_two)
    d_middle = out_grad.astype(f32) + d_middle_part
    d_attn = d_middle.astype(bf16)
    d_mixed = rounded(nt(d_attn, full_output))
    o_output = scattered(tn(mixed, d_attn))
    _, pull = jax.vjp(head_mix, attended, out_gate, gain_head)
    d_attended, d_out_gate, g_head = pull(d_mixed)
    d_att = d_attended.reshape(total, HEADS * DV)
    pulled = jnp.einsum(
        "mthv,mthc->mhvc",
        d_att.astype(bf16).reshape(micro, SLAB, HEADS, DV),
        reach_heads,
        preferred_element_type=f32,
    )
    pulls = lax.all_gather(pulled.astype(bf16), "fsdp", axis=0)
    d_end = jnp.zeros((micro, HEADS, DV, DK), f32)
    for k in range(count - 1, 0, -1):
        d_end = jnp.where(k > place, coefs[k] * d_end + pulls[k].astype(f32), d_end)
    d_query, d_key, d_value, d_log = core_behind(
        spans, queries, keys_in, values, log_gate, same, keep, tail,
        enters, enter_coefs, state_in, d_att, d_end,
    )
    d_pre = d_log / 16.0 * jax.nn.sigmoid(-gate_pre)
    g_bias = jnp.sum(d_pre, axis=0)
    d_pre_low = d_pre.astype(bf16)
    g_rank_out = tn(rank_mid, d_pre_low)
    d_rank = nt(d_pre_low, full_rank_out).astype(bf16)
    d_project = jnp.concatenate(
        [
            d_query,
            d_key,
            d_value,
            d_out_gate.astype(bf16),
            jnp.pad(d_rank, ((0, 0), (0, wide_rank - rank))),
        ],
        axis=1,
    )
    o_project = scattered(tn(normed, d_project))
    d_normed = rounded(nt(d_project, project))
    _, pull = jax.vjp(rms_scale, inputs, gain_one)
    d_input_part, g_norm = pull(d_normed)
    input_grad = d_middle + d_input_part

    few = jnp.concatenate(
        [
            g_norm.reshape(count, -1),
            g_bias.reshape(count, -1),
            g_head.reshape(count, -1),
            g_ffn.reshape(count, -1),
            g_rank_out.reshape(rank, count, -1).transpose(1, 0, 2).reshape(count, -1),
        ],
        axis=1,
    )
    few = lax.psum(few, ("dp", "fsdp"))
    few = lax.dynamic_index_in_dim(few, place, 0, False)
    s_norm, s_bias, s_head, s_ffn, s_rank_out = (few[cuts[n] : cuts[n + 1]] for n in range(5))
    s_down = across(o_down)
    s_pair = across(o_pair)
    s_output = across(o_output)
    s_project = across(o_project)
    return (
        block_out,
        input_grad,
        s_norm,
        s_project[:, :nq],
        s_project[:, nq : 2 * nq],
        s_project[:, 2 * nq : 2 * nq + nv],
        s_project[:, 2 * nq + 2 * nv : 2 * nq + 2 * nv + rank],
        s_rank_out.reshape(rank, -1),
        s_bias,
        s_project[:, 2 * nq + nv : 2 * nq + 2 * nv],
        s_head,
        s_output,
        s_ffn,
        s_pair[:, :ff],
        s_pair[:, ff:],
        s_down,
    )


def solution(mesh):
    return jax.shard_map(
        on_device,
        mesh=mesh,
        in_specs=(
            P(("dp", "fsdp"), None),
            P(("dp", "fsdp")),
            P(("dp", "fsdp"), None),
            P("fsdp"),
            P("fsdp", None),
            P("fsdp", None),
            P("fsdp", None),
            P("fsdp", None),
            P(None, "fsdp"),
            P("fsdp"),
            P("fsdp", None),
            P("fsdp"),
            P("fsdp", None),
            P("fsdp"),
            P("fsdp", None),
            P("fsdp", None),
            P("fsdp", None),
        ),
        out_specs=(
            P(("dp", "fsdp"), None),
            P(("dp", "fsdp"), None),
            P("fsdp"),
            P("fsdp", None),
            P("fsdp", None),
            P("fsdp", None),
            P("fsdp", None),
            P(None, "fsdp"),
            P("fsdp"),
            P("fsdp", None),
            P("fsdp"),
            P("fsdp", None),
            P("fsdp"),
            P("fsdp", None),
            P("fsdp", None),
            P("fsdp", None),
        ),
        check_vma=False,
    )
```

```python
import functools

import jax
import jax.numpy as jnp
import numpy as np
from jax import lax
from jax.experimental import pallas as pl
from jax.experimental.pallas import tpu as pltpu
from jax.sharding import PartitionSpec as P

HEADS = 4
DK = 128
DV = 256
SLAB = 384
CHUNK = 128
LEVELS = 7
SCALE = DK ** (-0.5)

eps_norm = 1e-06
eps_head = 0.1
bf16 = jnp.bfloat16
f32 = jnp.float32


def nn(left, right):
    return lax.dot_general(
        left.astype(bf16), right.astype(bf16), (((1,), (0,)), ((), ())), preferred_element_type=f32
    )


def tn(left, right):
    return lax.dot_general(
        left.astype(bf16), right.astype(bf16), (((0,), (0,)), ((), ())), preferred_element_type=f32
    )


def nt(left, right):
    return lax.dot_general(
        left.astype(bf16), right.astype(bf16), (((1,), (1,)), ((), ())), preferred_element_type=f32
    )


def rounded(values):
    return lax.optimization_barrier(values.astype(bf16)).astype(f32)


def rms_scale(values, gain):
    return values * lax.rsqrt(jnp.mean(values * values, axis=-1, keepdims=True) + eps_norm) * gain


def head_mix(attended, out_gate, head_gain):
    length = attended.shape[0]
    head_scale = lax.rsqrt(jnp.mean(attended * attended, axis=-1, keepdims=True) + eps_head)
    return (attended * head_scale * head_gain).reshape(length, -1) * jax.nn.silu(out_gate)


def swiglu(gate, upward):
    return jax.nn.silu(gate) * upward


def span_matrix():
    i = np.arange(CHUNK)[:, None]
    s = np.arange(CHUNK)[None, :]
    rows = []
    for level in range(LEVELS):
        half = 1 << level
        mid = (i // (2 * half)) * 2 * half + half - 1
        second = (i >> level) & 1 == 1
        rows.append(np.where(second, (s > mid) & (s <= i), (s > i) & (s <= mid)))
    rows.append(s <= i)
    rows.append(s > i)
    return np.concatenate(rows, axis=0).astype(np.float32)


def part(level):
    return slice(level * CHUNK, (level + 1) * CHUNK)


def chunk_factors(spans, g):
    high = g.astype(bf16)
    low = g - high.astype(f32)
    return jnp.exp(nn(spans, high) + nn(spans, low))


def iotas():
    return (
        lax.broadcasted_iota(jnp.int32, (CHUNK, CHUNK), 0),
        lax.broadcasted_iota(jnp.int32, (CHUNK, CHUNK), 1),
    )


def second_half(level, rows):
    return ((rows >> level) & 1) == 1


def meets(level, rows, columns):
    return ((rows >> (level + 1)) == (columns >> (level + 1))) & (
        (rows >> level) != (columns >> level)
    )


def chunk_scores(q, k, factors, same, rows, columns):
    scores = jnp.where(rows == columns, jnp.sum(q * k, axis=1, keepdims=True), 0.0)
    for level in range(LEVELS):
        mixed = (jnp.where(second_half(level, rows), q, k) * factors[part(level)]).astype(bf16)
        scores = scores + jnp.where(
            meets(level, rows, columns) & (rows > columns), nt(mixed, mixed), 0.0
        )
    return scores * same


def ahead_kernel(
    spans_ref,
    q_ref,
    k_ref,
    v_ref,
    g_ref,
    same_ref,
    keep_ref,
    tail_ref,
    out_ref,
    reach_ref,
    enter_ref,
    enter_coef_ref,
    last_ref,
    coef_ref,
    state,
    decay,
):
    step = pl.program_id(2)

    @pl.when(step == 0)
    def _():
        state[...] = jnp.zeros_like(state)
        decay[...] = jnp.ones_like(decay)

    rows, columns = iotas()
    q = q_ref[...].astype(f32) * SCALE
    k = k_ref[...].astype(f32)
    v = v_ref[...]
    factors = chunk_factors(spans_ref[...], g_ref[...])
    scores = chunk_scores(q, k, factors, same_ref[...].astype(f32), rows, columns)
    carry = factors[part(LEVELS)] * keep_ref[...].astype(f32)
    reach = q * carry
    tail = k * factors[part(LEVELS + 1)] * tail_ref[...].astype(f32)
    before = state[...]
    entering = decay[0:1, :]
    enter_ref[...] = before
    enter_coef_ref[...] = decay[...]
    out_ref[...] = nn(scores, v) + nt(reach, before)
    reach_ref[...] = (reach * entering).astype(bf16)
    coef = carry[CHUNK - 1 : CHUNK, :]
    after = before * coef + tn(v, tail)
    state[...] = after
    decay[...] = decay[...] * coef
    last_ref[...] = after
    coef_ref[...] = decay[...]


def behind_kernel(
    spans_ref,
    q_ref,
    k_ref,
    v_ref,
    g_ref,
    same_ref,
    keep_ref,
    tail_ref,
    enter_ref,
    enter_coef_ref,
    first_ref,
    grad_ref,
    end_ref,
    dq_ref,
    dk_ref,
    dv_ref,
    dg_ref,
    state,
    spread,
):
    step = pl.program_id(2)

    @pl.when(step == 0)
    def _():
        state[...] = end_ref[...]

    rows, columns = iotas()
    q = q_ref[...].astype(f32) * SCALE
    k = k_ref[...].astype(f32)
    v = v_ref[...]
    same = same_ref[...].astype(f32)
    factors = chunk_factors(spans_ref[...], g_ref[...])
    scores = chunk_scores(q, k, factors, same, rows, columns)
    carry = factors[part(LEVELS)] * keep_ref[...].astype(f32)
    reach = q * carry
    leave = factors[part(LEVELS + 1)] * tail_ref[...].astype(f32)
    tail = k * leave
    coef = carry[CHUNK - 1 : CHUNK, :]
    before = enter_ref[...] + enter_coef_ref[0:1, :] * first_ref[...]
    d_out = grad_ref[...].astype(bf16)
    d_after = state[...]

    d_scores = nt(d_out, v) * same
    dv_ref[...] = (tn(scores, d_out) + nt(tail, d_after)).astype(bf16)
    d_reach = nn(d_out, before)
    d_tail = nn(v, d_after)
    d_coef = jnp.sum(d_after * before, axis=0, keepdims=True)
    state[...] = coef * d_after + tn(d_out, reach)

    below = jnp.where(rows > columns, d_scores, 0.0)
    both = below + below.T
    diagonal = jnp.sum(jnp.where(rows == columns, d_scores, 0.0), axis=1, keepdims=True)
    d_q = diagonal * k + d_reach * carry
    d_k = diagonal * q + d_tail * leave
    for level in range(LEVELS):
        second = second_half(level, rows)
        factor = factors[part(level)]
        mixed = jnp.where(second, q, k) * factor
        d_mixed = nn(jnp.where(meets(level, rows, columns), both, 0.0), mixed)
        spread[part(level), :] = (d_mixed * mixed).astype(bf16)
        d_base = d_mixed * factor
        d_q = d_q + jnp.where(second, d_base, 0.0)
        d_k = d_k + jnp.where(second, 0.0, d_base)
    ending = jnp.where(rows == CHUNK - 1, d_coef * coef, 0.0)
    spread[part(LEVELS), :] = (d_reach * reach + ending).astype(bf16)
    spread[part(LEVELS + 1), :] = (d_tail * tail).astype(bf16)
    dg_ref[...] = tn(spans_ref[...], spread[...])
    dq_ref[...] = (d_q * SCALE).astype(bf16)
    dk_ref[...] = d_k.astype(bf16)


def core_specs(chunks, turn):
    def at(m, c):
        return m * chunks + turn(c)

    key = pl.BlockSpec((CHUNK, DK), lambda m, h, c: (at(m, c), h))
    value = pl.BlockSpec((CHUNK, DV), lambda m, h, c: (at(m, c), h))
    plain = pl.BlockSpec((CHUNK, CHUNK), lambda m, h, c: (at(m, c), 0))
    spans = pl.BlockSpec(((LEVELS + 2) * CHUNK, CHUNK), lambda m, h, c: (0, 0))
    enter = pl.BlockSpec((None, None, DV, DK), lambda m, h, c: (at(m, c), h, 0, 0))
    enter_coef = pl.BlockSpec((None, None, 8, DK), lambda m, h, c: (at(m, c), h, 0, 0))
    ends = pl.BlockSpec((None, None, DV, DK), lambda m, h, c: (m, h, 0, 0))
    coef = pl.BlockSpec((None, None, 8, DK), lambda m, h, c: (m, h, 0, 0))
    return key, value, plain, spans, enter, enter_coef, ends, coef


LIMIT = 32 * 1024 * 1024


def core_ahead(spans, q, k, v, g, same, keep, tail):
    total = q.shape[0]
    micro, chunks = total // SLAB, SLAB // CHUNK
    key, value, plain, span, enter, enter_coef, ends, coef = core_specs(chunks, lambda c: c)
    return pl.pallas_call(
        ahead_kernel,
        grid=(micro, HEADS, chunks),
        in_specs=[span, key, key, value, key, plain, plain, plain],
        out_specs=[value, key, enter, enter_coef, ends, coef],
        out_shape=[
            jax.ShapeDtypeStruct((total, HEADS * DV), f32),
            jax.ShapeDtypeStruct((total, HEADS * DK), bf16),
            jax.ShapeDtypeStruct((micro * chunks, HEADS, DV, DK), f32),
            jax.ShapeDtypeStruct((micro * chunks, HEADS, 8, DK), f32),
            jax.ShapeDtypeStruct((micro, HEADS, DV, DK), f32),
            jax.ShapeDtypeStruct((micro, HEADS, 8, DK), f32),
        ],
        scratch_shapes=[pltpu.VMEM((DV, DK), f32), pltpu.VMEM((8, DK), f32)],
        compiler_params=pltpu.CompilerParams(vmem_limit_bytes=LIMIT),
        cost_estimate=pl.CostEstimate(
            flops=12 * total * HEADS * 9 * CHUNK * DK // 2, bytes_accessed=20 * 2**20, transcendentals=0
        ),
        name="core_ahead",
    )(spans, q, k, v, g, same, keep, tail)


def core_behind(spans, q, k, v, g, same, keep, tail, enters, enter_coefs, first, d_out, d_end):
    total = q.shape[0]
    micro, chunks = total // SLAB, SLAB // CHUNK
    key, value, plain, span, enter, enter_coef, ends, coef = core_specs(
        chunks, lambda c: chunks - 1 - c
    )
    return pl.pallas_call(
        behind_kernel,
        grid=(micro, HEADS, chunks),
        in_specs=[span, key, key, value, key, plain, plain, plain]
        + [enter, enter_coef, ends, value, ends],
        out_specs=[key, key, value, key],
        out_shape=[
            jax.ShapeDtypeStruct((total, HEADS * DK), bf16),
            jax.ShapeDtypeStruct((total, HEADS * DK), bf16),
            jax.ShapeDtypeStruct((total, HEADS * DV), bf16),
            jax.ShapeDtypeStruct((total, HEADS * DK), f32),
        ],
        scratch_shapes=[
            pltpu.VMEM((DV, DK), f32),
            pltpu.VMEM(((LEVELS + 2) * CHUNK, DK), bf16),
        ],
        compiler_params=pltpu.CompilerParams(vmem_limit_bytes=LIMIT),
        cost_estimate=pl.CostEstimate(
            flops=24 * total * HEADS * 9 * CHUNK * DK // 2, bytes_accessed=24 * 2**20, transcendentals=0
        ),
        name="core_behind",
    )(spans, q, k, v, g, same, keep, tail, enters, enter_coefs, first, d_out, d_end)


def split_masks(seg, joined):
    micro = seg.shape[0] // SLAB
    chunks = SLAB // CHUNK
    rows = seg.reshape(micro, chunks, CHUNK)
    first = rows[:, 0, 0]
    enter_id = jnp.concatenate(
        [jnp.where(joined, first, -1)[:, None], rows[:, :-1, CHUNK - 1]], axis=1
    )
    keep = rows == enter_id[:, :, None]
    tail = rows == rows[:, :, CHUNK - 1 :]
    same = rows[:, :, :, None] == rows[:, :, None, :]

    def wide(mask):
        return jnp.broadcast_to(mask.astype(bf16).reshape(-1, 1), (seg.shape[0], DK))

    return same.astype(bf16).reshape(-1, CHUNK), wide(keep), wide(tail)


def gathered_rows(x):
    return lax.all_gather(x, "fsdp", axis=0, tiled=True)


def scattered(x):
    return lax.psum_scatter(x.astype(bf16), "fsdp", scatter_dimension=0, tiled=True)


def across(x):
    size = lax.axis_size("dp")
    hop = 1
    while hop < size:
        other = lax.ppermute(x, "dp", [(i, i ^ hop) for i in range(size)])
        whole = x.astype(f32) + other.astype(f32)
        x = whole.astype(bf16)
        hop *= 2
    return whole


def pack_state(coef, state):
    high = lax.optimization_barrier(coef.astype(bf16))
    low = (coef - high.astype(f32)).astype(bf16)
    return jnp.concatenate([a.astype(bf16).reshape(-1, DK) for a in (state, high, low)], axis=0)


def moved(coef, state, hop):
    size = lax.axis_size("fsdp")
    pairs = [(i, i + hop) for i in range(size) if 0 <= i + hop < size]
    parcel = lax.ppermute(pack_state(coef, state), "fsdp", pairs).astype(f32)
    lines, rows = coef.size // DK, state.size // DK
    new_coef = parcel[rows : rows + lines] + parcel[rows + lines :]
    return new_coef.reshape(coef.shape), parcel[:rows].reshape(state.shape)


def entering(coef, state, sign):
    coef, state = moved(coef, state, sign)
    hop = 1
    while hop < lax.axis_size("fsdp"):
        other_coef, other_state = moved(coef, state, sign * hop)
        state = coef * other_state + state
        coef = coef * other_coef
        hop *= 2
    return state


def on_device(
    tokens,
    segment_ids,
    out_grad,
    norm_gain,
    w_query,
    w_key,
    w_value,
    w_rank_in,
    w_rank_out,
    gate_bias,
    w_out_gate,
    head_gain,
    w_output,
    ffn_gain,
    w_gate,
    w_up,
    w_down,
):
    total = tokens.shape[0]
    micro = total // SLAB
    count, place = lax.axis_size("fsdp"), lax.axis_index("fsdp")
    owned_rows = norm_gain.shape[0]
    nq, nv, rank = w_query.shape[1], w_value.shape[1], w_rank_in.shape[1]
    ff = w_gate.shape[1]
    wide_rank = 128
    spans = jnp.asarray(span_matrix(), bf16)

    sizes = [a.size for a in (norm_gain, gate_bias, head_gain, ffn_gain, w_rank_out)]
    cuts = np.cumsum([0] + sizes)
    small = jnp.concatenate(
        [norm_gain, gate_bias, head_gain, ffn_gain, w_rank_out.reshape(-1)]
    )
    few_wide = -(-small.shape[0] // owned_rows)
    small = jnp.pad(small, (0, owned_rows * few_wide - small.shape[0])).reshape(owned_rows, few_wide)
    base = 2 * nq + 2 * nv
    blank = jnp.zeros((owned_rows, wide_rank - rank - few_wide), bf16)
    project = gathered_rows(
        jnp.concatenate([w_query, w_key, w_value, w_out_gate, w_rank_in, small, blank], axis=1)
    )
    small = project[:, base + rank : base + rank + few_wide].reshape(count, -1)
    full_norm, full_bias, full_head, full_ffn = (
        small[:, cuts[n] : cuts[n + 1]].reshape(-1) for n in range(4)
    )
    full_rank_out = (
        small[:, cuts[4] : cuts[5]].reshape(count, rank, -1).transpose(1, 0, 2).reshape(rank, -1)
    )
    project, w_output, w_gate, w_up, w_down = lax.optimization_barrier(
        (project, w_output, w_gate, w_up, w_down)
    )
    full_output = gathered_rows(w_output)
    full_pair = gathered_rows(jnp.concatenate([w_gate, w_up], axis=1))
    full_down = gathered_rows(w_down)

    inputs = tokens.astype(f32)
    gain_one = full_norm.astype(f32)
    normed = rms_scale(inputs, gain_one).astype(bf16)
    qkv = nn(normed, project[:, : 2 * nq + nv]).astype(bf16)
    queries, keys_in, values = qkv[:, :nq], qkv[:, nq : 2 * nq], qkv[:, 2 * nq :]
    rest = nn(normed, project[:, 2 * nq + nv :])
    out_gate = rest[:, :nv]
    rank_mid = rest[:, nv : nv + rank].astype(bf16)
    gate_pre = nn(rank_mid, full_rank_out) + full_bias.astype(f32)
    log_gate = jax.nn.log_sigmoid(gate_pre) / 16.0

    same, keep, tail = split_masks(segment_ids, place > 0)
    local_out, reach, enters, enter_coefs, local_state, coef = core_ahead(
        spans, queries, keys_in, values, log_gate, same, keep, tail
    )
    coef = coef[:, :, 0:1, :]
    state_in = entering(coef, local_state, 1)
    reach_heads = reach.reshape(micro, SLAB, HEADS, DK)
    carried = jnp.einsum(
        "mthc,mhvc->mthv", reach_heads, state_in.astype(bf16), preferred_element_type=f32
    )
    attended = local_out.reshape(total, HEADS, DV) + carried.reshape(total, HEADS, DV)
    gain_head = full_head.astype(f32)
    mixed = head_mix(attended, out_gate, gain_head).astype(bf16)
    middle = inputs + nn(mixed, full_output)
    gain_two = full_ffn.astype(f32)
    normed_two = rms_scale(middle, gain_two).astype(bf16)
    gate = nn(normed_two, full_pair[:, :ff])
    upward = nn(normed_two, full_pair[:, ff:])
    hidden = swiglu(gate, upward).astype(bf16)
    block_out = (middle + nn(hidden, full_down)).astype(bf16)

    d_branch = out_grad
    o_down = scattered(tn(hidden, d_branch))
    d_hidden = rounded(nt(d_branch, full_down))
    _, pull = jax.vjp(swiglu, gate, upward)
    d_pair = jnp.concatenate([a.astype(bf16) for a in pull(d_hidden)], axis=1)
    o_pair = scattered(tn(normed_two, d_pair))
    d_normed_two = rounded(nt(d_pair, full_pair))
    _, pull = jax.vjp(rms_scale, middle, gain_two)
    d_middle_part, g_ffn = pull(d_normed_two)
    d_middle = out_grad.astype(f32) + d_middle_part
    d_attn = d_middle.astype(bf16)
    d_mixed = rounded(nt(d_attn, full_output))
    o_output = scattered(tn(mixed, d_attn))
    _, pull = jax.vjp(head_mix, attended, out_gate, gain_head)
    d_attended, d_out_gate, g_head = pull(d_mixed)
    d_att = d_attended.reshape(total, HEADS * DV)
    pulled = jnp.einsum(
        "mthv,mthc->mhvc",
        d_att.astype(bf16).reshape(micro, SLAB, HEADS, DV),
        reach_heads,
        preferred_element_type=f32,
    )
    d_end = entering(coef, pulled, -1)
    d_query, d_key, d_value, d_log = core_behind(
        spans, queries, keys_in, values, log_gate, same, keep, tail,
        enters, enter_coefs, state_in, d_att, d_end,
    )
    d_pre = d_log / 16.0 * jax.nn.sigmoid(-gate_pre)
    g_bias = jnp.sum(d_pre, axis=0)
    d_pre_low = d_pre.astype(bf16)
    g_rank_out = tn(rank_mid, d_pre_low)
    d_rank = nt(d_pre_low, full_rank_out).astype(bf16)
    d_project = jnp.concatenate(
        [
            d_query,
            d_key,
            d_value,
            d_out_gate.astype(bf16),
            jnp.pad(d_rank, ((0, 0), (0, wide_rank - rank))),
        ],
        axis=1,
    )
    g_project = tn(normed, d_project)
    d_normed = rounded(nt(d_project, project))
    _, pull = jax.vjp(rms_scale, inputs, gain_one)
    d_input_part, g_norm = pull(d_normed)
    input_grad = d_middle + d_input_part

    few = jnp.concatenate(
        [
            g_norm.reshape(count, -1),
            g_bias.reshape(count, -1),
            g_head.reshape(count, -1),
            g_ffn.reshape(count, -1),
            g_rank_out.reshape(rank, count, -1).transpose(1, 0, 2).reshape(count, -1),
        ],
        axis=1,
    )
    few = jnp.pad(few, ((0, 0), (0, owned_rows * few_wide - few.shape[1])))
    few = few.reshape(count * owned_rows, few_wide)
    o_project = scattered(
        jnp.concatenate(
            [g_project[:, : base + rank], few, g_project[:, base + rank + few_wide :]], axis=1
        )
    )
    s_project = across(o_project)
    few = s_project[:, base + rank : base + rank + few_wide].reshape(-1)
    s_norm, s_bias, s_head, s_ffn, s_rank_out = (few[cuts[n] : cuts[n + 1]] for n in range(5))
    s_down = across(o_down)
    s_pair = across(o_pair)
    s_output = across(o_output)
    return (
        block_out,
        input_grad,
        s_norm,
        s_project[:, :nq],
        s_project[:, nq : 2 * nq],
        s_project[:, 2 * nq : 2 * nq + nv],
        s_project[:, 2 * nq + 2 * nv : 2 * nq + 2 * nv + rank],
        s_rank_out.reshape(rank, -1),
        s_bias,
        s_project[:, 2 * nq + nv : 2 * nq + 2 * nv],
        s_head,
        s_output,
        s_ffn,
        s_pair[:, :ff],
        s_pair[:, ff:],
        s_down,
    )


def solution(mesh):
    return jax.shard_map(
        on_device,
        mesh=mesh,
        in_specs=(
            P(("dp", "fsdp"), None),
            P(("dp", "fsdp")),
            P(("dp", "fsdp"), None),
            P("fsdp"),
            P("fsdp", None),
            P("fsdp", None),
            P("fsdp", None),
            P("fsdp", None),
            P(None, "fsdp"),
            P("fsdp"),
            P("fsdp", None),
            P("fsdp"),
            P("fsdp", None),
            P("fsdp"),
            P("fsdp", None),
            P("fsdp", None),
            P("fsdp", None),
        ),
        out_specs=(
            P(("dp", "fsdp"), None),
            P(("dp", "fsdp"), None),
            P("fsdp"),
            P("fsdp", None),
            P("fsdp", None),
            P("fsdp", None),
            P("fsdp", None),
            P(None, "fsdp"),
            P("fsdp"),
            P("fsdp", None),
            P("fsdp"),
            P("fsdp", None),
            P("fsdp"),
            P("fsdp", None),
            P("fsdp", None),
            P("fsdp", None),
        ),
        check_vma=False,
    )
```
